32 devices in a mesh: dp: 2 (over core), expert: 8 (over z, x), replica: 2 (over y).
Axes of the slice: x: 2, y: 2, z: 4, core: 2. Of those that a mesh axis runs over, the one named last changes fastest.
Arguments:
- tokens: bfloat16 [4096, 4096], P(('dp', 'expert', 'replica')), may hold values from -6 to 6
- expert_ids: int32 [4096, 8], P(('dp', 'expert', 'replica')), may hold values from 0 to 15, all different within a row; in each aligned block of 128 rows (0 to 127, 128 to 255, ...) at most 96 rows name the same one
- router_weight: bfloat16 [4096, 16], replicated, may hold values from -0.09375 to 0.09375
- gate_weight: bfloat16 [16, 4096, 768], P(('expert', 'replica')), may hold values from -0.09375 to 0.09375
- up_weight: bfloat16 [16, 4096, 768], P(('expert', 'replica')), may hold values from -0.09375 to 0.09375
- down_weight: bfloat16 [16, 768, 4096], P(('expert', 'replica')), may hold values from -0.21875 to 0.21875
- cotangent: bfloat16 [4096, 4096], P(('dp', 'expert', 'replica')), may hold values from -0.09375 to 0.09375
Outputs:
- mixed: bfloat16 [4096, 4096], P(('dp', 'expert', 'replica'))
- router_grad: float32 [4096, 16], replicated
The draws below stay inside these ranges and needn't reach their ends.
Inputs may be any that keep to these rules, and one draw needn't show every extreme that they name: `expert_ids`: in each aligned block of 128 rows (the rows of one device) no expert is named by more than 96 rows, and in every draw some expert is named by exactly 96 rows of some block.
All inputs are finite; a program needn't handle non-finite values.
Results may differ from the reference program's by a relative error of at most 0.0057.
Values may be sent and summed in bfloat16 or wider, within the bound.
A program may use at most 128 MiB of HBM per device.

```python
import math
import jax
import jax.numpy as jnp
import numpy as np
from jax import lax

D = 4096
FFE = 768
TOPK = 8
TOK_DEV = 128
E = 16
CAP = 96
TOKENS = 4096


def levels(rng, shape, shards, smallest, largest):
    loudness, own = 1.0, jax.random.fold_in(rng, 6)
    for position, shards_of in shards:
        draws = jnp.exp(jax.random.uniform(jax.random.fold_in(own, position), (shards_of,), jnp.float32, smallest / len(shards), largest / len(shards)))
        loudness = loudness * jnp.repeat(draws, shape[position] // shards_of).reshape([-1 if axis == position else 1 for axis in range(len(shape))])
    return loudness


def routed_block(rng, own, number, rows, count, top, reach, lean):
    sequence = jax.random.permutation(rng, count)
    crowded, usual = portions_of(count, rows * top, reach, lean, True), portions_of(count, rows * top, reach, lean, False)
    places = jnp.arange(count)

    def named(lengths, turn):
        used = int((lengths > 0).sum())
        fixed = max(1, used // 4)
        moved = fixed + (places - fixed + turn * (used - fixed)) % max(1, count - fixed)
        return jnp.zeros((count,), jnp.int32).at[sequence[jnp.where(places < fixed, places, moved)]].set(jnp.asarray(lengths, jnp.int32))

    lengths = jnp.where(number % 4 == 0, named(crowded, number // 4), named(usual, number - number // 4 - 1))
    mixed = jax.random.permutation(jax.random.fold_in(own, 3), count)
    donor, receiver = mixed[0:count // 2 * 2:2], mixed[1:count // 2 * 2:2]
    margin = jnp.minimum(lengths[donor] - 1, reach - lengths[receiver]) // 2
    margin = jnp.where((donor == sequence[0]) | (receiver == sequence[0]) | (lengths[receiver] == 0), 0, jnp.maximum(margin, 0))
    moved = jax.random.randint(jax.random.fold_in(own, 4), (count // 2,), 0, 1 << 20) % (margin + 1)
    lengths = lengths.at[donor].add(-moved).at[receiver].add(moved)
    items = jnp.searchsorted(jnp.cumsum(lengths), jnp.arange(rows * top), side="right").astype(jnp.int32)
    grid = items.reshape(top, rows).T
    grid = grid[jax.random.permutation(jax.random.fold_in(own, 1), rows)]
    turn = jax.random.randint(jax.random.fold_in(own, 2), (rows, 1), 0, top)
    return jnp.take_along_axis(grid, (jnp.arange(top)[None, :] + turn) % top, axis=1)


def portions_of(amount, total, limit, slope, full):
    portions = [(1 << 20) // math.isqrt(grade ** slope) + 1 for grade in range(1, amount + 1)]
    largest = limit if full else min(limit, max(-(-total // amount), total * portions[0] // sum(portions)))
    least = 1 if total - largest >= amount - 1 else 0
    given, rest = [largest] + [least] * (amount - 1), total - largest - least * (amount - 1)
    while rest > 0:
        movable = [i for i in range(1, amount) if given[i] < largest] or [i for i in range(1, amount) if given[i] < limit]
        whole, remaining = sum([portions[i] for i in movable]), rest
        for i in movable:
            more = min(limit - given[i], max(1, remaining * portions[i] // whole), rest)
            given[i] = given[i] + more
            rest = rest - more
    return np.array(given)


def normal_values(own_key, extent, spread, bound, shards=(), dtype=jnp.bfloat16):
    values = jax.random.normal(own_key, extent, jnp.float32) * spread
    if len(shards) > 0:
        values = levels(own_key, extent, shards, -0.22, 0.18) * values
    return jnp.clip(values, min=-bound, max=bound).astype(dtype)


def setup_inputs(seed: int = 0) -> dict:
    seeds = jax.random.split(jax.random.key(seed), 8)
    tokens = normal_values(seeds[0], (TOKENS, D), 1.0, 6.0, ((0, 32),))
    expert_ids_keys = jax.random.split(jax.random.fold_in(seeds[1], 1), TOKENS // TOK_DEV)
    expert_ids_turns = jax.random.permutation(jax.random.fold_in(seeds[1], 3), TOKENS // TOK_DEV)
    expert_ids = jax.vmap(lambda own, number: routed_block(jax.random.fold_in(seeds[1], 2), own, number, TOK_DEV, E, TOPK, CAP, 2))(expert_ids_keys, expert_ids_turns).reshape((TOKENS, TOPK))
    router_weight = normal_values(seeds[2], (D, E), D ** -0.5, 0.09375)
    gate_weight = normal_values(seeds[3], (E, D, FFE), D ** -0.5, 0.09375, ((0, 16),))
    up_weight = normal_values(seeds[4], (E, D, FFE), D ** -0.5, 0.09375, ((0, 16),))
    down_weight = normal_values(seeds[5], (E, FFE, D), FFE ** -0.5, 0.21875, ((0, 16),))
    cotangent = normal_values(seeds[6], (TOKENS, D), D ** -0.5, 0.09375, ((0, 32),))
    return dict(tokens=tokens, expert_ids=expert_ids, router_weight=router_weight, gate_weight=gate_weight, up_weight=up_weight, down_weight=down_weight, cotangent=cotangent)


def reference(tokens, expert_ids, router_weight, gate_weight, up_weight, down_weight, cotangent):
    logits = jnp.dot(tokens, router_weight, preferred_element_type=jnp.float32)
    chosen = jnp.take_along_axis(logits, expert_ids, axis=1)
    raised = jnp.exp(chosen)
    gate_probs = raised / jnp.sum(raised, axis=1, keepdims=True)
    flat_ids = expert_ids.reshape(-1)
    flat_probs = gate_probs.reshape(-1)
    row_bound = (TOKENS // TOK_DEV) * CAP

    def per_expert(carry, expert):
        mixed_acc, dot_acc = carry
        matches = flat_ids == expert
        (picked_idx,) = jnp.nonzero(matches, size=row_bound, fill_value=0)
        live_mask = (jnp.arange(row_bound) < jnp.sum(matches)).astype(jnp.float32)
        token_idx = picked_idx // TOPK
        picked = tokens[token_idx]
        gate_act = jnp.dot(picked, gate_weight[expert], preferred_element_type=jnp.float32)
        up_act = jnp.dot(picked, up_weight[expert], preferred_element_type=jnp.float32)
        hidden = (jax.nn.silu(gate_act) * up_act).astype(jnp.bfloat16)
        slot_out = jnp.dot(hidden, down_weight[expert], preferred_element_type=jnp.float32).astype(jnp.bfloat16)
        out_wide = slot_out.astype(jnp.float32)
        scale_rows = flat_probs[picked_idx] * live_mask
        mixed_acc = mixed_acc.at[token_idx].add(scale_rows[:, None] * out_wide)
        dot_rows = jnp.sum(out_wide * cotangent[token_idx].astype(jnp.float32), axis=1) * live_mask
        dot_acc = dot_acc.at[picked_idx].add(dot_rows)
        return (mixed_acc, dot_acc), None

    start = (jnp.zeros((TOKENS, D), jnp.float32), jnp.zeros((TOKENS * TOPK,), jnp.float32))
    (mixed_acc, dot_acc), _ = lax.scan(per_expert, start, jnp.arange(E).astype(jnp.int32))
    mixed = mixed_acc.astype(jnp.bfloat16)
    slot_dots = dot_acc.reshape(TOKENS, TOPK)
    logit_grad = gate_probs * (slot_dots - jnp.sum(gate_probs * slot_dots, axis=1, keepdims=True))
    match_table = (expert_ids[:, :, None] == jnp.arange(E).astype(jnp.int32)[None, None, :]).astype(jnp.float32)
    grad_table = jnp.sum(match_table * logit_grad[:, :, None], axis=1)
    router_grad = jnp.dot(tokens.astype(jnp.float32).T, grad_table, precision=lax.Precision.HIGHEST)
    return mixed, router_grad
```

```python
import jax
import jax.numpy as jnp
from jax import lax
from jax.sharding import PartitionSpec as P

GROUP = ("expert", "replica")


def split_three(wide):
    high = wide.astype(jnp.bfloat16)
    rest = wide - high.astype(jnp.float32)
    middle = rest.astype(jnp.bfloat16)
    low = (rest - middle.astype(jnp.float32)).astype(jnp.bfloat16)
    return jnp.concatenate([high, middle, low], axis=1)


def one_chunk(tokens, expert_ids, router_weight, gate_mat, up_mat, down_mat, cotangent):
    experts = router_weight.shape[1]
    me = lax.axis_index(GROUP)
    all_tokens = lax.all_gather(tokens, GROUP, axis=0, tiled=True)
    all_ids = lax.all_gather(expert_ids, GROUP, axis=0, tiled=True)
    all_cot = lax.all_gather(cotangent, GROUP, axis=0, tiled=True)
    logits = jnp.dot(all_tokens, router_weight, preferred_element_type=jnp.float32)
    columns = jnp.arange(experts, dtype=jnp.int32)
    chosen = jnp.any(all_ids[:, :, None] == columns[None, None, :], axis=1)
    raised = jnp.where(chosen, jnp.exp(logits), 0.0)
    probs = raised / jnp.sum(raised, axis=1, keepdims=True)
    mine = jnp.sum(jnp.where(columns[None, :] == me, probs, 0.0), axis=1, keepdims=True)
    gate_act = jnp.dot(all_tokens, gate_mat, preferred_element_type=jnp.float32)
    up_act = jnp.dot(all_tokens, up_mat, preferred_element_type=jnp.float32)
    hidden = (jax.nn.silu(gate_act) * up_act).astype(jnp.bfloat16)
    out = jnp.dot(hidden, down_mat, preferred_element_type=jnp.float32).astype(jnp.bfloat16)
    out = out.astype(jnp.float32)
    dots = jnp.sum(out * all_cot.astype(jnp.float32), axis=1)
    part = jnp.where(mine > 0, mine * out, 0.0).astype(jnp.bfloat16)
    mixed = lax.psum_scatter(part, GROUP, scatter_dimension=0, tiled=True)
    slot_dots = lax.all_gather(dots, GROUP, axis=0).T
    slot_dots = jnp.where(chosen, slot_dots, 0.0)
    grad_table = probs * (slot_dots - jnp.sum(probs * slot_dots, axis=1, keepdims=True))
    pieces = lax.dot_general(
        all_tokens, split_three(grad_table), (((0,), (0,)), ((), ())), preferred_element_type=jnp.float32
    )
    grad = pieces[:, :experts] + pieces[:, experts : 2 * experts] + pieces[:, 2 * experts :]
    return mixed, grad


def local(tokens, expert_ids, router_weight, gate_weight, up_weight, down_weight, cotangent):
    rows, width = tokens.shape
    experts = router_weight.shape[1]
    chunks = max(1, experts // 16)
    mats = (gate_weight[0], up_weight[0], down_weight[0])
    if chunks == 1:
        mixed, grad = one_chunk(tokens, expert_ids, router_weight, *mats, cotangent)
    else:

        def step(total, chunk):
            mixed, grad = one_chunk(chunk[0], chunk[1], router_weight, *mats, chunk[2])
            return total + grad, mixed

        cut = lambda full: full.reshape(chunks, rows // chunks, full.shape[1])
        grad, mixed = lax.scan(
            step,
            jnp.zeros((width, experts), jnp.float32),
            (cut(tokens), cut(expert_ids), cut(cotangent)),
        )
        mixed = mixed.reshape(rows, width)
    other = lax.ppermute(grad, "dp", [(0, 1), (1, 0)])
    first = lax.axis_index("dp") == 0
    router_grad = jnp.where(first, grad, other) + jnp.where(first, other, grad)
    return (mixed, router_grad)


def solution(mesh):
    in_specs = (
        P(("dp", "expert", "replica"), None),
        P(("dp", "expert", "replica"), None),
        P(),
        P(("expert", "replica"), None, None),
        P(("expert", "replica"), None, None),
        P(("expert", "replica"), None, None),
        P(("dp", "expert", "replica"), None),
    )
    out_specs = (P(("dp", "expert", "replica"), None), P())
    return jax.shard_map(local, mesh=mesh, in_specs=in_specs, out_specs=out_specs, check_vma=False)
```

```python
import jax
import jax.numpy as jnp
from jax import lax
from jax.sharding import PartitionSpec as P

GROUP = ("expert", "replica")


def split_three(wide):
    high = wide.astype(jnp.bfloat16)
    rest = wide - high.astype(jnp.float32)
    middle = rest.astype(jnp.bfloat16)
    low = (rest - middle.astype(jnp.float32)).astype(jnp.bfloat16)
    return jnp.concatenate([high, middle, low], axis=1)


def one_chunk(tokens, expert_ids, router_weight, gate_mat, up_mat, down_mat, cotangent):
    experts = router_weight.shape[1]
    me = lax.axis_index(GROUP)
    all_tokens = lax.all_gather(tokens, GROUP, axis=0, tiled=True)
    all_ids = lax.all_gather(expert_ids, GROUP, axis=0, tiled=True)
    all_cot = lax.all_gather(cotangent, GROUP, axis=0, tiled=True)
    logits = jnp.dot(all_tokens, router_weight, preferred_element_type=jnp.float32)
    columns = jnp.arange(experts, dtype=jnp.int32)
    chosen = jnp.any(all_ids[:, :, None] == columns[None, None, :], axis=1)
    raised = jnp.where(chosen, jnp.exp(logits), 0.0)
    probs = raised / jnp.sum(raised, axis=1, keepdims=True)
    mine = jnp.sum(jnp.where(columns[None, :] == me, probs, 0.0), axis=1, keepdims=True)
    gate_act = jnp.dot(all_tokens, gate_mat, preferred_element_type=jnp.float32)
    up_act = jnp.dot(all_tokens, up_mat, preferred_element_type=jnp.float32)
    hidden = (jax.nn.silu(gate_act) * up_act).astype(jnp.bfloat16)
    out = jnp.dot(hidden, down_mat, preferred_element_type=jnp.float32).astype(jnp.bfloat16)
    out = out.astype(jnp.float32)
    dots = jnp.sum(out * all_cot.astype(jnp.float32), axis=1)
    part = jnp.where(mine > 0, mine * out, 0.0).astype(jnp.bfloat16)
    mixed = lax.psum_scatter(part, GROUP, scatter_dimension=0, tiled=True)
    slot_dots = lax.all_gather(dots, GROUP, axis=0).T
    slot_dots = jnp.where(chosen, slot_dots, 0.0)
    grad_table = probs * (slot_dots - jnp.sum(probs * slot_dots, axis=1, keepdims=True))
    pieces = lax.dot_general(
        all_tokens, split_three(grad_table), (((0,), (0,)), ((), ())), preferred_element_type=jnp.float32
    )
    grad = pieces[:, :experts] + pieces[:, experts : 2 * experts] + pieces[:, 2 * experts :]
    return mixed, grad


def paired(tokens, expert_ids, router_weight, gate_weight, up_weight, down_weight, cotangent, layers):
    rows, width = tokens.shape
    experts = router_weight.shape[1]
    units = gate_weight.shape[2]
    place = lax.axis_index("expert")
    layer, side = place // 2, place % 2
    copy = lax.axis_index("replica")
    core = lax.axis_index("dp")
    half = units // 2

    def shift(block, step):
        pairs = [(z * 2 + x, (z + step) % layers * 2 + x) for z in range(layers) for x in range(2)]
        return lax.ppermute(block, "expert", pairs)

    def swap(block):
        return lax.ppermute(block, "expert", [(e, e ^ 1) for e in range(2 * layers)])

    def across(block, axis):
        return lax.ppermute(block, axis, [(0, 1), (1, 0)])

    def spread(block):
        near = [block] + [shift(block, step) for step in range(1, layers)]
        return [near, [swap(one) for one in near]]

    first_half = core * half
    sent = (
        lax.dynamic_slice(gate_weight[0], (0, first_half), (width, half)),
        lax.dynamic_slice(up_weight[0], (0, first_half), (width, half)),
        lax.dynamic_slice(down_weight[0], (first_half, 0), (half, width)),
    )
    fetched = [across(part, "replica") for part in sent]
    second = [
        jnp.concatenate([part, across(part, "dp")], axis=axis) for part, axis in zip(fetched, (1, 1, 0))
    ]
    mats = [(gate_weight[0], up_weight[0], down_weight[0]), tuple(second)]

    logits = jnp.dot(tokens, router_weight, preferred_element_type=jnp.float32)
    columns = jnp.arange(experts, dtype=jnp.int32)
    chosen = jnp.any(expert_ids[:, :, None] == columns[None, None, :], axis=1)
    raised = jnp.where(chosen, jnp.exp(logits), 0.0)
    own_probs = raised / jnp.sum(raised, axis=1, keepdims=True)

    token_blocks = spread(tokens)
    prob_blocks = spread(own_probs)
    cotangent, _ = lax.optimization_barrier((cotangent, token_blocks[0][layers - 1]))
    cot_blocks = spread(cotangent)
    token_sides = [jnp.concatenate(blocks, axis=0) for blocks in token_blocks]
    prob_sides = [jnp.concatenate(blocks, axis=0) for blocks in prob_blocks]
    cot_sides = [jnp.concatenate(blocks, axis=0) for blocks in cot_blocks]

    def expert_on(which, x):
        gate_mat, up_mat, down_mat = mats[which]
        gate_act = jnp.dot(token_sides[x], gate_mat, preferred_element_type=jnp.float32)
        up_act = jnp.dot(token_sides[x], up_mat, preferred_element_type=jnp.float32)
        hidden = (jax.nn.silu(gate_act) * up_act).astype(jnp.bfloat16)
        out = jnp.dot(hidden, down_mat, preferred_element_type=jnp.float32).astype(jnp.bfloat16)
        out = out.astype(jnp.float32)
        name = place * 2 + (copy if which == 0 else 1 - copy)
        mine = jnp.sum(jnp.where(columns[None, :] == name, prob_sides[x], 0.0), axis=1, keepdims=True)
        return mine * out, jnp.sum(out * cot_sides[x].astype(jnp.float32), axis=1)

    own = [expert_on(0, x) for x in range(2)]
    other = [None, None]
    other[1] = expert_on(1, 1)
    far = (own[1][0] + other[1][0]).astype(jnp.bfloat16).reshape(layers, rows, width)
    arrived = [swap(far[step]) for step in range(layers)]
    other[0] = expert_on(1, 0)
    near = (own[0][0] + other[0][0]).reshape(layers, rows, width)
    sums = [near[step] + arrived[step].astype(jnp.float32) for step in range(layers)]
    mixed = sums[0]
    for step in range(1, layers):
        mixed = mixed + shift(sums[step].astype(jnp.bfloat16), -step).astype(jnp.float32)
    mixed = mixed.astype(jnp.bfloat16)

    dots = jnp.stack(
        [jnp.stack([own[x][1] for x in range(2)]), jnp.stack([other[x][1] for x in range(2)])]
    ).reshape(2, 2, layers, rows)
    dot_blocks = spread(dots.reshape(4 * layers, rows))
    table = jnp.zeros((2 * layers * rows, experts), jnp.float32)
    for x in range(2):
        for step in range(layers):
            block = dot_blocks[x][step].reshape(2, 2, layers, rows)
            block = jnp.roll(jnp.flip(block, 1) if x else block, step, axis=2).reshape(2, -1)
            there = ((layer - step) % layers * 2 + (side ^ x)) * 2
            for which in range(2):
                name = there + (copy if which == 0 else 1 - copy)
                table = jnp.where(columns[None, :] == name, block[which][:, None], table)
    probs = jnp.concatenate(prob_sides, axis=0)
    grad_table = probs * (table - jnp.sum(probs * table, axis=1, keepdims=True))
    part = width // (2 * layers)
    strip = jnp.concatenate(
        [lax.dynamic_slice(side_rows, (0, place * part), (layers * rows, part)) for side_rows in token_sides]
    )
    pieces = lax.dot_general(
        strip, split_three(grad_table), (((0,), (0,)), ((), ())), preferred_element_type=jnp.float32
    )
    grad = pieces[:, :experts] + pieces[:, experts : 2 * experts] + pieces[:, 2 * experts :]
    grad = grad + across(grad, "replica")
    grad = grad + across(grad, "dp")
    strips = jnp.stack([jnp.stack(blocks) for blocks in spread(grad.reshape(part * experts // 128, 128))])
    whose = jnp.arange(2 * layers, dtype=jnp.int32)
    from_side, from_layer = (whose % 2) ^ side, (layer - whose // 2) % layers
    router_grad = strips.reshape(2 * layers, -1)[from_side * layers + from_layer].reshape(width, experts)
    return mixed, router_grad


def local(tokens, expert_ids, router_weight, gate_weight, up_weight, down_weight, cotangent):
    rows, width = tokens.shape
    experts = router_weight.shape[1]
    if lax.axis_size("expert") == 8 and lax.axis_size("replica") == 2:
        return paired(
            tokens, expert_ids, router_weight, gate_weight, up_weight, down_weight, cotangent, 4
        )
    chunks = max(1, experts // 16)
    mats = (gate_weight[0], up_weight[0], down_weight[0])
    if chunks == 1:
        mixed, grad = one_chunk(tokens, expert_ids, router_weight, *mats, cotangent)
    else:

        def step(total, chunk):
            mixed, grad = one_chunk(chunk[0], chunk[1], router_weight, *mats, chunk[2])
            return total + grad, mixed

        cut = lambda full: full.reshape(chunks, rows // chunks, full.shape[1])
        grad, mixed = lax.scan(
            step,
            jnp.zeros((width, experts), jnp.float32),
            (cut(tokens), cut(expert_ids), cut(cotangent)),
        )
        mixed = mixed.reshape(rows, width)
    other = lax.ppermute(grad, "dp", [(0, 1), (1, 0)])
    first = lax.axis_index("dp") == 0
    router_grad = jnp.where(first, grad, other) + jnp.where(first, other, grad)
    return (mixed, router_grad)


def solution(mesh):
    in_specs = (
        P(("dp", "expert", "replica"), None),
        P(("dp", "expert", "replica"), None),
        P(),
        P(("expert", "replica"), None, None),
        P(("expert", "replica"), None, None),
        P(("expert", "replica"), None, None),
        P(("dp", "expert", "replica"), None),
    )
    out_specs = (P(("dp", "expert", "replica"), None), P())
    return jax.shard_map(local, mesh=mesh, in_specs=in_specs, out_specs=out_specs, check_vma=False)
```

```python
import jax
import jax.numpy as jnp
from jax import lax
from jax.sharding import PartitionSpec as P

GROUP = ("expert", "replica")


def split_three(wide):
    high = wide.astype(jnp.bfloat16)
    rest = wide - high.astype(jnp.float32)
    middle = rest.astype(jnp.bfloat16)
    low = (rest - middle.astype(jnp.float32)).astype(jnp.bfloat16)
    return jnp.concatenate([high, middle, low], axis=1)


def one_chunk(tokens, expert_ids, router_weight, gate_mat, up_mat, down_mat, cotangent):
    experts = router_weight.shape[1]
    me = lax.axis_index(GROUP)
    all_tokens = lax.all_gather(tokens, GROUP, axis=0, tiled=True)
    all_ids = lax.all_gather(expert_ids, GROUP, axis=0, tiled=True)
    all_cot = lax.all_gather(cotangent, GROUP, axis=0, tiled=True)
    logits = jnp.dot(all_tokens, router_weight, preferred_element_type=jnp.float32)
    columns = jnp.arange(experts, dtype=jnp.int32)
    chosen = jnp.any(all_ids[:, :, None] == columns[None, None, :], axis=1)
    raised = jnp.where(chosen, jnp.exp(logits), 0.0)
    probs = raised / jnp.sum(raised, axis=1, keepdims=True)
    mine = jnp.sum(jnp.where(columns[None, :] == me, probs, 0.0), axis=1, keepdims=True)
    gate_act = jnp.dot(all_tokens, gate_mat, preferred_element_type=jnp.float32)
    up_act = jnp.dot(all_tokens, up_mat, preferred_element_type=jnp.float32)
    hidden = (jax.nn.silu(gate_act) * up_act).astype(jnp.bfloat16)
    out = jnp.dot(hidden, down_mat, preferred_element_type=jnp.float32).astype(jnp.bfloat16)
    out = out.astype(jnp.float32)
    dots = jnp.sum(out * all_cot.astype(jnp.float32), axis=1)
    part = jnp.where(mine > 0, mine * out, 0.0).astype(jnp.bfloat16)
    mixed = lax.psum_scatter(part, GROUP, scatter_dimension=0, tiled=True)
    slot_dots = lax.all_gather(dots, GROUP, axis=0).T
    slot_dots = jnp.where(chosen, slot_dots, 0.0)
    grad_table = probs * (slot_dots - jnp.sum(probs * slot_dots, axis=1, keepdims=True))
    pieces = lax.dot_general(
        all_tokens, split_three(grad_table), (((0,), (0,)), ((), ())), preferred_element_type=jnp.float32
    )
    grad = pieces[:, :experts] + pieces[:, experts : 2 * experts] + pieces[:, 2 * experts :]
    return mixed, grad


def paired(tokens, expert_ids, router_weight, gate_weight, up_weight, down_weight, cotangent, layers):
    rows, width = tokens.shape
    experts = router_weight.shape[1]
    units = gate_weight.shape[2]
    place = lax.axis_index("expert")
    layer, side = place // 2, place % 2
    copy = lax.axis_index("replica")
    core = lax.axis_index("dp")
    half = units // 2

    def shift(block, step):
        pairs = [(z * 2 + x, (z + step) % layers * 2 + x) for z in range(layers) for x in range(2)]
        return lax.ppermute(block, "expert", pairs)

    def swap(block):
        return lax.ppermute(block, "expert", [(e, e ^ 1) for e in range(2 * layers)])

    def across(block, axis):
        return lax.ppermute(block, axis, [(0, 1), (1, 0)])

    def follow(block, after):
        return block if after is None else lax.optimization_barrier((block, after))[0]

    def spread(block, shifts, swaps):
        near = [block] + [shift(follow(block, shifts.get(step)), step) for step in range(1, layers)]
        return [near, [swap(follow(one, swaps.get(step))) for step, one in enumerate(near)]]

    first_half = core * half
    sent = (
        lax.dynamic_slice(gate_weight[0], (0, first_half), (width, half)),
        lax.dynamic_slice(up_weight[0], (0, first_half), (width, half)),
        lax.dynamic_slice(down_weight[0], (first_half, 0), (half, width)),
    )
    fetched = [across(sent[0], "replica"), None, across(sent[2], "replica")]
    later, _ = lax.optimization_barrier((sent[1], fetched[2]))
    fetched[1] = across(later, "replica")
    second = [
        jnp.concatenate([part, across(part, "dp")], axis=axis) for part, axis in zip(fetched, (1, 1, 0))
    ]
    mats = [(gate_weight[0], up_weight[0], down_weight[0]), tuple(second)]

    columns = jnp.arange(experts, dtype=jnp.int32)
    chosen = jnp.any(expert_ids[:, :, None] == columns[None, None, :], axis=1)
    marks = jnp.pad(chosen.astype(jnp.bfloat16), ((0, 0), (0, -experts % 128)))
    marked = jnp.concatenate([tokens, marks], axis=1)
    marked, _ = lax.optimization_barrier((marked, sent[2]))
    token_blocks = spread(marked, {}, {})
    cotangent = follow(cotangent, (token_blocks[0], fetched[2]))
    cot_blocks = spread(
        cotangent, {layers - 1: fetched[0]}, {0: token_blocks[1], layers - 1: fetched[1]}
    )

    def in_order(blocks, start, size):
        whole = jnp.zeros((layers * rows, size), blocks[0].dtype)
        for step, block in enumerate(blocks):
            at = (layer - step) % layers * rows
            whole = lax.dynamic_update_slice(whole, block[:, start : start + size], (at, 0))
        return whole

    def cut(whole, step):
        return lax.dynamic_slice(whole, ((layer - step) % layers * rows, 0), (rows, width))

    token_sides = [in_order(blocks, 0, width) for blocks in token_blocks]
    mark_sides = [in_order(blocks, width, experts) for blocks in token_blocks]
    cot_sides = [in_order(blocks, 0, width) for blocks in cot_blocks]

    both = jnp.concatenate(token_sides, axis=0)
    logits = jnp.dot(both, router_weight, preferred_element_type=jnp.float32)
    raised = jnp.where(jnp.concatenate(mark_sides, axis=0) > 0, jnp.exp(logits), 0.0)
    probs = raised / jnp.sum(raised, axis=1, keepdims=True)
    prob_sides = jnp.split(probs, 2, axis=0)

    def expert_on(which, x, rows_in, after=None):
        gate_mat, up_mat, down_mat = mats[which]
        gate_act = jnp.dot(rows_in, gate_mat, preferred_element_type=jnp.float32)
        up_act = jnp.dot(rows_in, up_mat, preferred_element_type=jnp.float32)
        hidden = follow((jax.nn.silu(gate_act) * up_act).astype(jnp.bfloat16), after)
        out = jnp.dot(hidden, down_mat, preferred_element_type=jnp.float32).astype(jnp.bfloat16)
        out = out.astype(jnp.float32)
        name = place * 2 + (copy if which == 0 else 1 - copy)
        mine = jnp.sum(jnp.where(columns[None, :] == name, prob_sides[x], 0.0), axis=1, keepdims=True)
        return mine * out, jnp.sum(out * cot_sides[x].astype(jnp.float32), axis=1)

    own = [expert_on(0, x, follow(token_sides[x], fetched[2])) for x in range(2)]
    other = [None, None]
    other[1] = expert_on(1, 1, token_sides[1])
    far = (own[1][0] + other[1][0]).astype(jnp.bfloat16)
    first = [1, layers - 1]
    rest = list(range(2, layers - 1)) + [0]
    far_blocks = {step: cut(far, step) for step in first + rest}
    held, far_blocks = lax.optimization_barrier((token_sides[0], far_blocks))
    arrived = {step: swap(far_blocks[step]) for step in first}
    other[0] = expert_on(1, 0, held, arrived[first[0]])
    near = own[0][0] + other[0][0]

    dots = jnp.stack([own[0][1], own[1][1], other[0][1], other[1][1]]).reshape(-1, 128)
    dot_near = jnp.concatenate([dots] + [shift(dots, step) for step in range(1, layers)], axis=0)
    dot_far = swap(dot_near)
    held_far, dot_far = lax.optimization_barrier(([far_blocks[step] for step in rest], dot_far))
    for step, block in zip(rest, held_far):
        arrived[step] = swap(block)

    mixed = None
    for step in first + rest:
        total = cut(near, step) + arrived[step].astype(jnp.float32)
        if step:
            total = shift(total.astype(jnp.bfloat16), -step).astype(jnp.float32)
        mixed = total if mixed is None else mixed + total
    mixed = mixed.astype(jnp.bfloat16)

    table = jnp.zeros((2 * layers * rows, experts), jnp.float32)
    for x, found in enumerate((dot_near, dot_far)):
        found = found.reshape(layers, 2, 2, layers * rows)
        if x:
            found = jnp.flip(found, 2)
        found = found.reshape(layers, 2, -1)
        for step in range(layers):
            there = ((layer - step) % layers * 2 + (side ^ x)) * 2
            for which in range(2):
                name = there + (copy if which == 0 else 1 - copy)
                table = jnp.where(columns[None, :] == name, found[step, which][:, None], table)
    grad_table = probs * (table - jnp.sum(probs * table, axis=1, keepdims=True))
    pieces = lax.dot_general(
        both.reshape(2, layers * rows, width),
        split_three(grad_table).reshape(2, layers * rows, 3 * experts),
        (((1,), (1,)), ((0,), (0,))),
        preferred_element_type=jnp.float32,
    )
    grads = pieces[:, :, :experts] + pieces[:, :, experts : 2 * experts] + pieces[:, :, 2 * experts :]
    grad = grads[0] + grads[1]
    grad = grad + across(grad, "replica")
    return mixed, grad + across(grad, "dp")


def local(tokens, expert_ids, router_weight, gate_weight, up_weight, down_weight, cotangent):
    rows, width = tokens.shape
    experts = router_weight.shape[1]
    if lax.axis_size("expert") == 8 and lax.axis_size("replica") == 2:
        return paired(
            tokens, expert_ids, router_weight, gate_weight, up_weight, down_weight, cotangent, 4
        )
    chunks = max(1, experts // 16)
    mats = (gate_weight[0], up_weight[0], down_weight[0])
    if chunks == 1:
        mixed, grad = one_chunk(tokens, expert_ids, router_weight, *mats, cotangent)
    else:

        def step(total, chunk):
            mixed, grad = one_chunk(chunk[0], chunk[1], router_weight, *mats, chunk[2])
            return total + grad, mixed

        cut = lambda full: full.reshape(chunks, rows // chunks, full.shape[1])
        grad, mixed = lax.scan(
            step,
            jnp.zeros((width, experts), jnp.float32),
            (cut(tokens), cut(expert_ids), cut(cotangent)),
        )
        mixed = mixed.reshape(rows, width)
    other = lax.ppermute(grad, "dp", [(0, 1), (1, 0)])
    first = lax.axis_index("dp") == 0
    router_grad = jnp.where(first, grad, other) + jnp.where(first, other, grad)
    return (mixed, router_grad)


def solution(mesh):
    in_specs = (
        P(("dp", "expert", "replica"), None),
        P(("dp", "expert", "replica"), None),
        P(),
        P(("expert", "replica"), None, None),
        P(("expert", "replica"), None, None),
        P(("expert", "replica"), None, None),
        P(("dp", "expert", "replica"), None),
    )
    out_specs = (P(("dp", "expert", "replica"), None), P())
    return jax.shard_map(local, mesh=mesh, in_specs=in_specs, out_specs=out_specs, check_vma=False)
```

```python
import jax
import jax.numpy as jnp
from jax import lax
from jax.sharding import PartitionSpec as P

GROUP = ("expert", "replica")


def split_three(wide):
    high = wide.astype(jnp.bfloat16)
    rest = wide - high.astype(jnp.float32)
    middle = rest.astype(jnp.bfloat16)
    low = (rest - middle.astype(jnp.float32)).astype(jnp.bfloat16)
    return jnp.concatenate([high, middle, low], axis=1)


def one_chunk(tokens, expert_ids, router_weight, gate_mat, up_mat, down_mat, cotangent):
    experts = router_weight.shape[1]
    me = lax.axis_index(GROUP)
    all_tokens = lax.all_gather(tokens, GROUP, axis=0, tiled=True)
    all_ids = lax.all_gather(expert_ids, GROUP, axis=0, tiled=True)
    all_cot = lax.all_gather(cotangent, GROUP, axis=0, tiled=True)
    logits = jnp.dot(all_tokens, router_weight, preferred_element_type=jnp.float32)
    columns = jnp.arange(experts, dtype=jnp.int32)
    chosen = jnp.any(all_ids[:, :, None] == columns[None, None, :], axis=1)
    raised = jnp.where(chosen, jnp.exp(logits), 0.0)
    probs = raised / jnp.sum(raised, axis=1, keepdims=True)
    mine = jnp.sum(jnp.where(columns[None, :] == me, probs, 0.0), axis=1, keepdims=True)
    gate_act = jnp.dot(all_tokens, gate_mat, preferred_element_type=jnp.float32)
    up_act = jnp.dot(all_tokens, up_mat, preferred_element_type=jnp.float32)
    hidden = (jax.nn.silu(gate_act) * up_act).astype(jnp.bfloat16)
    out = jnp.dot(hidden, down_mat, preferred_element_type=jnp.float32).astype(jnp.bfloat16)
    out = out.astype(jnp.float32)
    dots = jnp.sum(out * all_cot.astype(jnp.float32), axis=1)
    part = jnp.where(mine > 0, mine * out, 0.0).astype(jnp.bfloat16)
    mixed = lax.psum_scatter(part, GROUP, scatter_dimension=0, tiled=True)
    slot_dots = lax.all_gather(dots, GROUP, axis=0).T
    slot_dots = jnp.where(chosen, slot_dots, 0.0)
    grad_table = probs * (slot_dots - jnp.sum(probs * slot_dots, axis=1, keepdims=True))
    pieces = lax.dot_general(
        all_tokens, split_three(grad_table), (((0,), (0,)), ((), ())), preferred_element_type=jnp.float32
    )
    grad = pieces[:, :experts] + pieces[:, experts : 2 * experts] + pieces[:, 2 * experts :]
    return mixed, grad


def paired(tokens, expert_ids, router_weight, gate_weight, up_weight, down_weight, cotangent, layers):
    rows, width = tokens.shape
    experts = router_weight.shape[1]
    units = gate_weight.shape[2]
    place = lax.axis_index("expert")
    layer, side = place // 2, place % 2
    copy = lax.axis_index("replica")
    core = lax.axis_index("dp")
    half = units // 2

    def shift(block, step):
        pairs = [(z * 2 + x, (z + step) % layers * 2 + x) for z in range(layers) for x in range(2)]
        return lax.ppermute(block, "expert", pairs)

    def swap(block):
        return lax.ppermute(block, "expert", [(e, e ^ 1) for e in range(2 * layers)])

    def across(block, axis):
        return lax.ppermute(block, axis, [(0, 1), (1, 0)])

    def follow(block, after):
        return block if after is None else lax.optimization_barrier((block, after))[0]

    def spread(block, shifts, start, last=None):
        near = [block] + [shift(follow(block, shifts.get(step)), step) for step in range(1, layers)]
        far = []
        for step, one in enumerate(near):
            after = [far[step - 2] if step >= 2 else start, last if step == layers - 1 else None]
            far.append(swap(follow(one, [one for one in after if one is not None])))
        return [near, far]

    first_half = core * half
    sent = (
        lax.dynamic_slice(gate_weight[0], (0, first_half), (width, half)),
        lax.dynamic_slice(up_weight[0], (0, first_half), (width, half)),
        lax.dynamic_slice(down_weight[0], (first_half, 0), (half, width)),
    )
    fetched = {2: across(sent[2], "replica")}
    fetched[0] = across(sent[0], "replica")
    fetched[1] = across(follow(sent[1], fetched[2]), "replica")
    fetched = [fetched[which] for which in range(3)]
    second = [
        jnp.concatenate([part, across(part, "dp")], axis=axis) for part, axis in zip(fetched, (1, 1, 0))
    ]
    mats = [(gate_weight[0], up_weight[0], down_weight[0]), tuple(second)]

    columns = jnp.arange(experts, dtype=jnp.int32)
    chosen = jnp.any(expert_ids[:, :, None] == columns[None, None, :], axis=1)
    marks = jnp.pad(chosen.astype(jnp.bfloat16), ((0, 0), (0, -experts % 128)))
    marked = jnp.concatenate([tokens, marks], axis=1)
    marked, _ = lax.optimization_barrier((marked, sent[2]))
    token_blocks = spread(marked, {}, None, fetched[2])
    cotangent = follow(cotangent, (token_blocks[0], fetched[2]))
    cot_blocks = spread(cotangent, {layers - 1: fetched[0]}, token_blocks[1][layers - 1])
    cot_blocks[1][layers - 1] = follow(cot_blocks[1][layers - 1], fetched[1])

    def in_order(blocks, start, size):
        whole = jnp.zeros((layers * rows, size), blocks[0].dtype)
        for step, block in enumerate(blocks):
            at = (layer - step) % layers * rows
            whole = lax.dynamic_update_slice(whole, block[:, start : start + size], (at, 0))
        return whole

    def cut(whole, step):
        return lax.dynamic_slice(whole, ((layer - step) % layers * rows, 0), (rows, width))

    token_sides = [in_order(blocks, 0, width) for blocks in token_blocks]
    mark_sides = [in_order(blocks, width, experts) for blocks in token_blocks]
    cot_sides = [in_order(blocks, 0, width) for blocks in cot_blocks]

    both = jnp.concatenate(token_sides, axis=0)
    logits = jnp.dot(both, router_weight, preferred_element_type=jnp.float32)
    raised = jnp.where(jnp.concatenate(mark_sides, axis=0) > 0, jnp.exp(logits), 0.0)
    probs = raised / jnp.sum(raised, axis=1, keepdims=True)
    prob_sides = jnp.split(probs, 2, axis=0)

    def expert_on(which, x, rows_in, after=None):
        gate_mat, up_mat, down_mat = mats[which]
        gate_act = jnp.dot(rows_in, gate_mat, preferred_element_type=jnp.float32)
        up_act = jnp.dot(rows_in, up_mat, preferred_element_type=jnp.float32)
        hidden = follow((jax.nn.silu(gate_act) * up_act).astype(jnp.bfloat16), after)
        out = jnp.dot(hidden, down_mat, preferred_element_type=jnp.float32).astype(jnp.bfloat16)
        out = out.astype(jnp.float32)
        name = place * 2 + (copy if which == 0 else 1 - copy)
        mine = jnp.sum(jnp.where(columns[None, :] == name, prob_sides[x], 0.0), axis=1, keepdims=True)
        return mine * out, jnp.sum(out * cot_sides[x].astype(jnp.float32), axis=1)

    own = [expert_on(0, x, follow(token_sides[x], fetched[2])) for x in range(2)]
    other = [None, None]
    other[1] = expert_on(1, 1, token_sides[1])
    far = (own[1][0] + other[1][0]).astype(jnp.bfloat16)
    first = [2, 1]
    rest = [3, 0]
    far_blocks = {step: cut(far, step) for step in first + rest}
    held, far_blocks = lax.optimization_barrier((token_sides[0], far_blocks))
    arrived = {step: swap(far_blocks[step]) for step in first}
    other[0] = expert_on(1, 0, held, arrived[first[0]])
    near = own[0][0] + other[0][0]

    dots = jnp.stack([own[0][1], own[1][1], other[0][1], other[1][1]]).reshape(-1, 128)
    dot_near = jnp.concatenate([dots] + [shift(dots, step) for step in range(1, layers)], axis=0)
    dot_far = swap(dot_near)
    held_far, dot_far = lax.optimization_barrier(([far_blocks[step] for step in rest], dot_far))
    for step, block in zip(rest, held_far):
        arrived[step] = swap(block)

    mixed, before = None, None
    for step in first + rest:
        total = cut(near, step) + follow(arrived[step], before).astype(jnp.float32)
        if step:
            before = total.astype(jnp.bfloat16)
            total = shift(before, -step).astype(jnp.float32)
        mixed = total if mixed is None else mixed + total
    mixed = mixed.astype(jnp.bfloat16)

    table = jnp.zeros((2 * layers * rows, experts), jnp.float32)
    for x, found in enumerate((dot_near, dot_far)):
        found = found.reshape(layers, 2, 2, layers * rows)
        if x:
            found = jnp.flip(found, 2)
        found = found.reshape(layers, 2, -1)
        for step in range(layers):
            there = ((layer - step) % layers * 2 + (side ^ x)) * 2
            for which in range(2):
                name = there + (copy if which == 0 else 1 - copy)
                table = jnp.where(columns[None, :] == name, found[step, which][:, None], table)
    grad_table = probs * (table - jnp.sum(probs * table, axis=1, keepdims=True))
    pieces = lax.dot_general(
        both.reshape(2, layers * rows, width),
        split_three(grad_table).reshape(2, layers * rows, 3 * experts),
        (((1,), (1,)), ((0,), (0,))),
        preferred_element_type=jnp.float32,
    )
    grads = pieces[:, :, :experts] + pieces[:, :, experts : 2 * experts] + pieces[:, :, 2 * experts :]
    grad = grads[0] + grads[1]
    grad = grad + across(grad, "replica")
    return mixed, grad + across(grad, "dp")


def local(tokens, expert_ids, router_weight, gate_weight, up_weight, down_weight, cotangent):
    rows, width = tokens.shape
    experts = router_weight.shape[1]
    if lax.axis_size("expert") == 8 and lax.axis_size("replica") == 2:
        return paired(
            tokens, expert_ids, router_weight, gate_weight, up_weight, down_weight, cotangent, 4
        )
    chunks = max(1, experts // 16)
    mats = (gate_weight[0], up_weight[0], down_weight[0])
    if chunks == 1:
        mixed, grad = one_chunk(tokens, expert_ids, router_weight, *mats, cotangent)
    else:

        def step(total, chunk):
            mixed, grad = one_chunk(chunk[0], chunk[1], router_weight, *mats, chunk[2])
            return total + grad, mixed

        cut = lambda full: full.reshape(chunks, rows // chunks, full.shape[1])
        grad, mixed = lax.scan(
            step,
            jnp.zeros((width, experts), jnp.float32),
            (cut(tokens), cut(expert_ids), cut(cotangent)),
        )
        mixed = mixed.reshape(rows, width)
    other = lax.ppermute(grad, "dp", [(0, 1), (1, 0)])
    first = lax.axis_index("dp") == 0
    router_grad = jnp.where(first, grad, other) + jnp.where(first, other, grad)
    return (mixed, router_grad)


def solution(mesh):
    in_specs = (
        P(("dp", "expert", "replica"), None),
        P(("dp", "expert", "replica"), None),
        P(),
        P(("expert", "replica"), None, None),
        P(("expert", "replica"), None, None),
        P(("expert", "replica"), None, None),
        P(("dp", "expert", "replica"), None),
    )
    out_specs = (P(("dp", "expert", "replica"), None), P())
    return jax.shard_map(local, mesh=mesh, in_specs=in_specs, out_specs=out_specs, check_vma=False)
```

```python
import jax
import jax.numpy as jnp
from jax import lax
from jax.sharding import PartitionSpec as P

GROUP = ("expert", "replica")


def split_three(wide):
    high = wide.astype(jnp.bfloat16)
    rest = wide - high.astype(jnp.float32)
    middle = rest.astype(jnp.bfloat16)
    low = (rest - middle.astype(jnp.float32)).astype(jnp.bfloat16)
    return jnp.concatenate([high, middle, low], axis=1)


def one_chunk(tokens, expert_ids, router_weight, gate_mat, up_mat, down_mat, cotangent):
    experts = router_weight.shape[1]
    me = lax.axis_index(GROUP)
    all_tokens = lax.all_gather(tokens, GROUP, axis=0, tiled=True)
    all_ids = lax.all_gather(expert_ids, GROUP, axis=0, tiled=True)
    all_cot = lax.all_gather(cotangent, GROUP, axis=0, tiled=True)
    logits = jnp.dot(all_tokens, router_weight, preferred_element_type=jnp.float32)
    columns = jnp.arange(experts, dtype=jnp.int32)
    chosen = jnp.any(all_ids[:, :, None] == columns[None, None, :], axis=1)
    raised = jnp.where(chosen, jnp.exp(logits), 0.0)
    probs = raised / jnp.sum(raised, axis=1, keepdims=True)
    mine = jnp.sum(jnp.where(columns[None, :] == me, probs, 0.0), axis=1, keepdims=True)
    gate_act = jnp.dot(all_tokens, gate_mat, preferred_element_type=jnp.float32)
    up_act = jnp.dot(all_tokens, up_mat, preferred_element_type=jnp.float32)
    hidden = (jax.nn.silu(gate_act) * up_act).astype(jnp.bfloat16)
    out = jnp.dot(hidden, down_mat, preferred_element_type=jnp.float32).astype(jnp.bfloat16)
    out = out.astype(jnp.float32)
    dots = jnp.sum(out * all_cot.astype(jnp.float32), axis=1)
    part = jnp.where(mine > 0, mine * out, 0.0).astype(jnp.bfloat16)
    mixed = lax.psum_scatter(part, GROUP, scatter_dimension=0, tiled=True)
    slot_dots = lax.all_gather(dots, GROUP, axis=0).T
    slot_dots = jnp.where(chosen, slot_dots, 0.0)
    grad_table = probs * (slot_dots - jnp.sum(probs * slot_dots, axis=1, keepdims=True))
    pieces = lax.dot_general(
        all_tokens, split_three(grad_table), (((0,), (0,)), ((), ())), preferred_element_type=jnp.float32
    )
    grad = pieces[:, :experts] + pieces[:, experts : 2 * experts] + pieces[:, 2 * experts :]
    return mixed, grad


def paired(tokens, expert_ids, router_weight, gate_weight, up_weight, down_weight, cotangent, layers):
    rows, width = tokens.shape
    experts = router_weight.shape[1]
    units = gate_weight.shape[2]
    place = lax.axis_index("expert")
    layer, side = place // 2, place % 2
    copy = lax.axis_index("replica")
    core = lax.axis_index("dp")
    half = units // 2

    def shift(block, step):
        pairs = [(z * 2 + x, (z + step) % layers * 2 + x) for z in range(layers) for x in range(2)]
        return lax.ppermute(block, "expert", pairs)

    def swap(block):
        return lax.ppermute(block, "expert", [(e, e ^ 1) for e in range(2 * layers)])

    def across(block, axis):
        return lax.ppermute(block, axis, [(0, 1), (1, 0)])

    def follow(block, after):
        return block if after is None else lax.optimization_barrier((block, after))[0]

    def spread(block, shifts, start, last=None):
        near = [block] + [shift(follow(block, shifts.get(step)), step) for step in range(1, layers)]
        far = []
        for step, one in enumerate(near):
            after = [far[step - 2] if step >= 2 else start, last if step == layers - 1 else None]
            far.append(swap(follow(one, [one for one in after if one is not None])))
        return [near, far]

    first_half = core * half
    sent = (
        lax.dynamic_slice(gate_weight[0], (0, first_half), (width, half)),
        lax.dynamic_slice(up_weight[0], (0, first_half), (width, half)),
        lax.dynamic_slice(down_weight[0], (first_half, 0), (half, width)),
    )
    fetched = {2: across(sent[2], "replica")}
    fetched[0] = across(sent[0], "replica")
    fetched[1] = across(follow(sent[1], fetched[2]), "replica")
    fetched = [fetched[which] for which in range(3)]
    second = [
        jnp.concatenate([part, across(part, "dp")], axis=axis) for part, axis in zip(fetched, (1, 1, 0))
    ]
    mats = [(gate_weight[0], up_weight[0], down_weight[0]), tuple(second)]

    columns = jnp.arange(experts, dtype=jnp.int32)
    chosen = jnp.any(expert_ids[:, :, None] == columns[None, None, :], axis=1)
    marks = jnp.pad(chosen.astype(jnp.bfloat16), ((0, 0), (0, -experts % 128)))
    marked = jnp.concatenate([tokens, marks], axis=1)
    marked, _ = lax.optimization_barrier((marked, sent[2]))
    token_blocks = spread(marked, {}, None, fetched[2])
    cotangent = follow(cotangent, (token_blocks[0], fetched[2]))
    cot_blocks = spread(cotangent, {layers - 1: fetched[0]}, token_blocks[1][layers - 2])
    cot_blocks[1][layers - 1] = follow(cot_blocks[1][layers - 1], fetched[1])

    def in_order(blocks, start, size):
        whole = jnp.zeros((layers * rows, size), blocks[0].dtype)
        for step, block in enumerate(blocks):
            at = (layer - step) % layers * rows
            whole = lax.dynamic_update_slice(whole, block[:, start : start + size], (at, 0))
        return whole

    def cut(whole, step):
        return lax.dynamic_slice(whole, ((layer - step) % layers * rows, 0), (rows, width))

    token_sides = [in_order(blocks, 0, width) for blocks in token_blocks]
    mark_sides = [in_order(blocks, width, experts) for blocks in token_blocks]
    cot_sides = [in_order(blocks, 0, width) for blocks in cot_blocks]

    both = jnp.concatenate(token_sides, axis=0)
    logits = jnp.dot(both, router_weight, preferred_element_type=jnp.float32)
    raised = jnp.where(jnp.concatenate(mark_sides, axis=0) > 0, jnp.exp(logits), 0.0)
    probs = raised / jnp.sum(raised, axis=1, keepdims=True)
    prob_sides = jnp.split(probs, 2, axis=0)

    def expert_on(which, x, rows_in, after=None):
        gate_mat, up_mat, down_mat = mats[which]
        gate_act = jnp.dot(rows_in, gate_mat, preferred_element_type=jnp.float32)
        up_act = jnp.dot(rows_in, up_mat, preferred_element_type=jnp.float32)
        hidden = follow((jax.nn.silu(gate_act) * up_act).astype(jnp.bfloat16), after)
        out = jnp.dot(hidden, down_mat, preferred_element_type=jnp.float32).astype(jnp.bfloat16)
        out = out.astype(jnp.float32)
        name = place * 2 + (copy if which == 0 else 1 - copy)
        mine = jnp.sum(jnp.where(columns[None, :] == name, prob_sides[x], 0.0), axis=1, keepdims=True)
        return mine * out, jnp.sum(out * cot_sides[x].astype(jnp.float32), axis=1)

    own = [expert_on(0, x, follow(token_sides[x], fetched[2])) for x in range(2)]
    other = [None, None]
    other[1] = expert_on(1, 1, token_sides[1])
    far = (own[1][0] + other[1][0]).astype(jnp.bfloat16)
    first = [2, 1]
    rest = [3, 0]
    far_blocks = {step: cut(far, step) for step in first + rest}
    held, far_blocks = lax.optimization_barrier((token_sides[0], far_blocks))
    arrived = {step: swap(far_blocks[step]) for step in first}
    other[0] = expert_on(1, 0, held, arrived[first[0]])
    near = own[0][0] + other[0][0]

    dots = jnp.stack([own[0][1], own[1][1], other[0][1], other[1][1]]).reshape(-1, 128)
    dot_near = jnp.concatenate([dots] + [shift(dots, step) for step in range(1, layers)], axis=0)
    dot_far = swap(dot_near)
    held_far, dot_far = lax.optimization_barrier(([far_blocks[step] for step in rest], dot_far))
    for step, block in zip(rest, held_far):
        arrived[step] = swap(block)

    mixed, before = None, None
    for step in first + rest:
        total = cut(near, step) + follow(arrived[step], before).astype(jnp.float32)
        if step:
            before = total.astype(jnp.bfloat16)
            total = shift(before, -step).astype(jnp.float32)
        mixed = total if mixed is None else mixed + total
    mixed = mixed.astype(jnp.bfloat16)

    table = jnp.zeros((2 * layers * rows, experts), jnp.float32)
    for x, found in enumerate((dot_near, dot_far)):
        found = found.reshape(layers, 2, 2, layers * rows)
        if x:
            found = jnp.flip(found, 2)
        found = found.reshape(layers, 2, -1)
        for step in range(layers):
            there = ((layer - step) % layers * 2 + (side ^ x)) * 2
            for which in range(2):
                name = there + (copy if which == 0 else 1 - copy)
                table = jnp.where(columns[None, :] == name, found[step, which][:, None], table)
    grad_table = probs * (table - jnp.sum(probs * table, axis=1, keepdims=True))
    pieces = lax.dot_general(
        both.reshape(2, layers * rows, width),
        split_three(grad_table).reshape(2, layers * rows, 3 * experts),
        (((1,), (1,)), ((0,), (0,))),
        preferred_element_type=jnp.float32,
    )
    grads = pieces[:, :, :experts] + pieces[:, :, experts : 2 * experts] + pieces[:, :, 2 * experts :]
    grad = grads[0] + grads[1]
    grad = grad + across(grad, "replica")
    return mixed, grad + across(grad, "dp")


def local(tokens, expert_ids, router_weight, gate_weight, up_weight, down_weight, cotangent):
    rows, width = tokens.shape
    experts = router_weight.shape[1]
    if lax.axis_size("expert") == 8 and lax.axis_size("replica") == 2:
        return paired(
            tokens, expert_ids, router_weight, gate_weight, up_weight, down_weight, cotangent, 4
        )
    chunks = max(1, experts // 16)
    mats = (gate_weight[0], up_weight[0], down_weight[0])
    if chunks == 1:
        mixed, grad = one_chunk(tokens, expert_ids, router_weight, *mats, cotangent)
    else:

        def step(total, chunk):
            mixed, grad = one_chunk(chunk[0], chunk[1], router_weight, *mats, chunk[2])
            return total + grad, mixed

        cut = lambda full: full.reshape(chunks, rows // chunks, full.shape[1])
        grad, mixed = lax.scan(
            step,
            jnp.zeros((width, experts), jnp.float32),
            (cut(tokens), cut(expert_ids), cut(cotangent)),
        )
        mixed = mixed.reshape(rows, width)
    other = lax.ppermute(grad, "dp", [(0, 1), (1, 0)])
    first = lax.axis_index("dp") == 0
    router_grad = jnp.where(first, grad, other) + jnp.where(first, other, grad)
    return (mixed, router_grad)


def solution(mesh):
    in_specs = (
        P(("dp", "expert", "replica"), None),
        P(("dp", "expert", "replica"), None),
        P(),
        P(("expert", "replica"), None, None),
        P(("expert", "replica"), None, None),
        P(("expert", "replica"), None, None),
        P(("dp", "expert", "replica"), None),
    )
    out_specs = (P(("dp", "expert", "replica"), None), P())
    return jax.shard_map(local, mesh=mesh, in_specs=in_specs, out_specs=out_specs, check_vma=False)
```
